32 devices in a mesh: grp: 2 (over y), pair: 4 (over z), ga: 2 (over x), sub: 2 (over core).
Axes of the slice: x: 2, y: 2, z: 4, core: 2. Of those that a mesh axis runs over, the one named last changes fastest.
Arguments:
- densities: bfloat16 [256, 122880], P(('grp', 'pair'), 'ga'), parts along dimension 0, may hold values from -6 to 6
- eigvecs: bfloat16 [2, 61440, 2048], P('ga', 'pair', 'sub'), may hold values from -0.015625 to 0.015625
- energies: float32 [256], P('grp'), parts along dimension 0, may hold values from 0.1 to 2
- frequencies: float32 [4], replicated, may hold values from 0.05 to 2
Outputs:
- chi_sub: float32 [8, 2048, 2048], P('grp', 'sub', ('pair', 'ga')), parts along dimension 0
The draws below stay inside these ranges and needn't reach their ends.
There are 2 independent parts, one for each index of `grp`. The reference program is written for one: setup_inputs(seed, part) draws one part's arguments, and reference() takes and returns one part's arrays. A program takes and returns all parts, laid end to end along the dimension named above; an argument that names none is the same for every part. Nothing has to cross between parts.
All inputs are finite; a program needn't handle non-finite values.
Results may differ from the reference program's by a relative error of at most 0.0048.
Values may be sent and summed in bfloat16 or wider, within the bound.
A program may use at most 128 MiB of HBM per device.

```python
import math
import jax
import jax.numpy as jnp

NG = 122880
S = 2048
NW = 4
NP = 128
GSLAB = 61440
N_GA = 2


def block_levels(rng, shape, split, low, high):
    def one(dim, blocks):
        heights = jax.random.uniform(jax.random.fold_in(jax.random.fold_in(rng, 6), dim), (blocks,), jnp.float32, low / len(split), high / len(split))
        return jnp.repeat(jnp.exp(heights), shape[dim] // blocks).reshape((-1,) + (1,) * (len(shape) - dim - 1))

    factor_of = one(*split[0])
    for cut in split[1:]:
        factor_of = factor_of * one(*cut)
    return factor_of


def bell_draw(key, shape, deviation, reach, pieces=(), held_as=jnp.bfloat16):
    factor_of = block_levels(key, shape, pieces, -0.22, 0.18) if pieces else 1.0
    values = jax.random.normal(key, shape, jnp.float32) * deviation * factor_of
    return jnp.minimum(jnp.maximum(values, -reach), reach).astype(held_as)


def setup_inputs(seed: int = 0, part: int = 0) -> dict:
    key_list = jax.random.split(jax.random.key(seed), 5)
    part_splits = jax.random.split(jax.random.fold_in(key_list[4], part), 5)
    return {
        "densities": bell_draw(part_splits[0], (NP, NG), 1.0, 6.0, ((0, 4), (1, 2))),
        "eigvecs": bell_draw(key_list[1], (N_GA, GSLAB, S), NG ** -0.5, 0.015625, ((0, 2), (1, 4), (2, 2))),
        "energies": jnp.clip(jnp.exp(jax.random.uniform(part_splits[2], (NP,), jnp.float32, math.log(0.1), math.log(2.0))), 0.1, 2.0),
        "frequencies": jnp.clip(jnp.exp(jax.random.uniform(key_list[3], (NW,), jnp.float32, math.log(0.05), math.log(2.0))), 0.05, 2.0),
    }


def reference(densities, eigvecs, energies, frequencies):
    basis = eigvecs.reshape(NG, S)
    coef = jnp.dot(densities, basis, preferred_element_type=jnp.float32).astype(jnp.bfloat16)
    factor = 2.0 * energies[None, :] / (energies[None, :] * energies[None, :] + frequencies[:, None] * frequencies[:, None])
    weighted = (factor[:, :, None] * coef.astype(jnp.float32)[None, :, :]).astype(jnp.bfloat16)
    chi_sub = jnp.einsum("ps,wpt->wst", coef.astype(jnp.float32), weighted.astype(jnp.float32))
    return chi_sub * (-1.0 / NP)
```

```python
import functools

import jax
import jax.numpy as jnp
from jax import lax
from jax.experimental import pallas as pl
from jax.experimental.pallas import tpu as pltpu
from jax.sharding import PartitionSpec as P

MESH = pl.DeviceIdType.MESH
WIDTH = 1536
TILE = 256


def flipped(index, bits):
    bit = 1
    while bit <= bits:
        if bits & bit:
            index = index + bit - 2 * bit * ((index // bit) % 2)
        bit *= 2
    return index


def span(start, size, unit):
    return pl.ds(pl.multiple_of(start, unit), size)


def kernel(n, n_ga, chunks, with_tail, dens, basis, *refs):
    if with_tail:
        (coef_out, block_out, eig, exch, total, sums, coef, other,
         eig_sem, own_sem, send, recv, fwd_send, fwd_recv,
         sum_send, sum_recv, all_send, all_recv, sib_send, sib_recv) = refs
    else:
        total, eig, exch, eig_sem, own_sem, send, recv, fwd_send, fwd_recv = refs
    z, x, c = lax.axis_index("pair"), lax.axis_index("ga"), lax.axis_index("sub")
    depth, half = eig.shape
    rows = exch.shape[1]
    part = rows // 2
    width = depth // chunks
    groups = n * n_ga
    rank = z * n_ga + x
    pieced = len(dens.shape) == 3

    def cols(k):
        return slice(None) if chunks == 1 else span(k * width, width, 128)

    def eig_copy(k):
        at = span(k * width, width, 16)
        return pltpu.make_async_copy(basis.at[0, at], eig.at[at], eig_sem.at[k])

    def own_copy():
        src = dens.at[z] if pieced else dens.at[:, span(z * depth, depth, 128)]
        return pltpu.make_async_copy(src, exch.at[z], own_sem)

    mine = span(c * part, part, part)

    def sending(k, d):
        to = flipped(z, d)
        if pieced:
            src = dens.at[to, mine]
        else:
            src = dens.at[mine, span(to * depth + k * width, width, 128)]
        return pltpu.make_async_remote_copy(
            src_ref=src, dst_ref=exch.at[z, mine, cols(k)],
            send_sem=send.at[k, d - 1], recv_sem=recv.at[k, d - 1],
            device_id={"pair": to}, device_id_type=MESH)

    def forwarding(k, d):
        here = exch.at[flipped(z, d), mine, cols(k)]
        return pltpu.make_async_remote_copy(
            src_ref=here, dst_ref=here,
            send_sem=fwd_send.at[k, d - 1], recv_sem=fwd_recv.at[k, d - 1],
            device_id={"sub": 1 - c}, device_id_type=MESH)

    def peer(e):
        to = flipped(rank, e)
        return to, {"pair": to // n_ga, "ga": to % n_ga}

    def loop(count, body):
        lax.fori_loop(0, count, lambda i, _: (body(i), 0)[1], 0)

    loop(chunks, lambda k: eig_copy(k).start())
    own_copy().start()

    barrier = pltpu.get_barrier_semaphore()
    greeted = range(1, groups) if with_tail else range(n_ga, groups, n_ga)
    for e in greeted:
        pl.semaphore_signal(barrier, inc=1, device_id=peer(e)[1], device_id_type=MESH)
    pl.semaphore_signal(barrier, inc=1, device_id={"sub": 1 - c}, device_id_type=MESH)
    pl.semaphore_wait(barrier, len(greeted) + 1)

    far_first = range(n - 1, 0, -1)

    def send_chunk(k):
        for d in far_first:
            sending(k, d).start()

    loop(chunks, send_chunk)
    total[...] = jnp.zeros_like(total)
    own_copy().wait()

    def step(k):
        @pl.when(k < chunks)
        def _():
            for d in far_first:
                sending(k, d).wait_recv()
                forwarding(k, d).start()

        @pl.when(k > 0)
        def _():
            last = k - 1
            eig_copy(last).wait()
            for d in far_first:
                forwarding(last, d).wait_recv()
            left = exch[:, :, cols(last)].reshape(n * rows, width)

            def tile(j):
                at = span(j * TILE, TILE, TILE)
                total[:, at] += jnp.dot(
                    left, eig[span(last * width, width, 16), at],
                    preferred_element_type=jnp.float32)

            loop(half // TILE, tile)

    loop(chunks + 1, step)

    def drain(k):
        for d in far_first:
            sending(k, d).wait_send()
            forwarding(k, d).wait_send()

    if not with_tail:
        loop(chunks, drain)
        return

    share = n * rows // groups
    own_rows = span(rank * share, share, share)

    def summing(e):
        to, device = peer(e)
        return pltpu.make_async_remote_copy(
            src_ref=total.at[span(to * share, share, share)], dst_ref=sums.at[e - 1],
            send_sem=sum_send.at[e - 1], recv_sem=sum_recv.at[e - 1],
            device_id=device, device_id_type=MESH)

    def sharing(e):
        return pltpu.make_async_remote_copy(
            src_ref=coef.at[own_rows], dst_ref=coef.at[own_rows],
            send_sem=all_send.at[e - 1], recv_sem=all_recv.at[e - 1],
            device_id=peer(e)[1], device_id_type=MESH)

    for e in range(groups - 1, 0, -1):
        summing(e).start()
    loop(chunks, drain)
    acc = total[own_rows, :]
    for e in range(1, groups):
        summing(e).wait_recv()
        acc = acc + sums[e - 1]
    coef[own_rows, :] = acc.astype(jnp.bfloat16)
    for e in range(groups - 1, 0, -1):
        sharing(e).start()
    for e in range(1, groups):
        summing(e).wait_send()
    for e in range(1, groups):
        sharing(e).wait()

    block = 2 * half // groups
    per_half = groups // 2
    at = span((rank % per_half) * block, block, block)
    sibling = pltpu.make_async_remote_copy(
        src_ref=coef.at[:, at], dst_ref=other, send_sem=sib_send, recv_sem=sib_recv,
        device_id={"sub": 1 - c}, device_id_type=MESH)
    sibling.start()
    coef_out[...] = coef[...]
    sibling.wait()
    here = rank // per_half == c

    @pl.when(here)
    def _():
        block_out[...] = coef[:, at]

    @pl.when(jnp.logical_not(here))
    def _():
        block_out[...] = other[...]


def projected(densities, eigvecs, n, n_ga):
    rows = densities.shape[0]
    _, depth, half = eigvecs.shape
    groups = n * n_ga
    pairs = n * rows
    chunks = depth // WIDTH if depth % WIDTH == 0 else 1
    with_tail = (
        pairs % (16 * groups) == 0 and (2 * half) % (128 * groups) == 0 and groups % 2 == 0
    )
    if depth % 128:
        densities = densities.reshape(rows, n, depth).transpose(1, 0, 2)
    dma = pltpu.SemaphoreType.DMA
    any_space = pl.BlockSpec(memory_space=pl.ANY)
    vmem = pl.BlockSpec(memory_space=pltpu.VMEM)
    scratch = [pltpu.VMEM((depth, half), jnp.bfloat16), pltpu.VMEM((n, rows, depth), jnp.bfloat16)]
    sems = [dma((chunks,)), dma] + [dma((chunks, n - 1))] * 4
    if with_tail:
        share, block = pairs // groups, 2 * half // groups
        scratch += [
            pltpu.VMEM((pairs, half), jnp.float32),
            pltpu.VMEM((groups - 1, share, half), jnp.float32),
            pltpu.VMEM((pairs, half), jnp.bfloat16),
            pltpu.VMEM((pairs, block), jnp.bfloat16),
        ]
        sems += [dma((groups - 1,))] * 4 + [dma, dma]
        out_shape = (
            jax.ShapeDtypeStruct((pairs, half), jnp.bfloat16),
            jax.ShapeDtypeStruct((pairs, block), jnp.bfloat16),
        )
        out_specs = (vmem, vmem)
    else:
        out_shape = jax.ShapeDtypeStruct((pairs, half), jnp.float32)
        out_specs = vmem
    return with_tail, pl.pallas_call(
        functools.partial(kernel, n, n_ga, chunks, with_tail),
        out_shape=out_shape,
        in_specs=[any_space, any_space],
        out_specs=out_specs,
        scratch_shapes=scratch + sems,
        compiler_params=pltpu.CompilerParams(
            collective_id=0, has_side_effects=True, vmem_limit_bytes=56 * 1024 * 1024),
        cost_estimate=pl.CostEstimate(
            flops=2 * pairs * depth * half, transcendentals=0,
            bytes_accessed=2 * depth * (half + pairs)),
    )(densities, eigvecs)


def on_device(densities, eigvecs, energies, frequencies):
    n, n_ga = lax.axis_size("pair"), lax.axis_size("ga")
    total_pairs = n * densities.shape[0]
    done, got = projected(densities, eigvecs, n, n_ga)
    if done:
        coefficients, columns = got
    else:
        coefficients = lax.psum(got, ("pair", "ga")).astype(jnp.bfloat16)
        half = coefficients.shape[1]
        width = 2 * half // (n * n_ga)
        start = (lax.axis_index("pair") * n_ga + lax.axis_index("ga")) * width
        swapped = lax.ppermute(coefficients, "sub", [(0, 1), (1, 0)])
        first = lax.axis_index("sub") == 0
        whole = jnp.concatenate(
            [jnp.where(first, coefficients, swapped), jnp.where(first, swapped, coefficients)], axis=1)
        columns = lax.dynamic_slice_in_dim(whole, start, width, 1)
    squared = energies * energies
    factor = (
        2.0 * energies[None, :] / (squared[None, :] + frequencies[:, None] * frequencies[:, None])
    )
    weighted = (factor[:, :, None] * columns.astype(jnp.float32)[None, :, :]).astype(jnp.bfloat16)
    result = jnp.einsum("ps,wpt->wst", coefficients, weighted, preferred_element_type=jnp.float32)
    return result * (-1.0 / total_pairs)


def solution(mesh):
    placed = (P(("grp", "pair"), "ga"), P("ga", "pair", "sub"), P("grp"), P())
    return jax.shard_map(
        on_device,
        mesh=mesh,
        in_specs=placed,
        out_specs=P("grp", "sub", ("pair", "ga")),
        check_vma=False,
    )
```

```python
import functools

import jax
import jax.numpy as jnp
from jax import lax
from jax.experimental import pallas as pl
from jax.experimental.pallas import tpu as pltpu
from jax.sharding import PartitionSpec as P

MESH = pl.DeviceIdType.MESH
WIDTH = 1536
TILE = 256
STAGES = 2
AHEAD = 4


def flipped(index, bits):
    bit = 1
    while bit <= bits:
        if bits & bit:
            index = index + bit - 2 * bit * ((index // bit) % 2)
        bit *= 2
    return index


def span(start, size, unit):
    return pl.ds(pl.multiple_of(start, unit), size)


def plain_kernel(n, n_ga, dens, basis, total, eig, exch, eig_sem, own_sem, send, recv, fwd_send, fwd_recv):
    z, x, c = lax.axis_index("pair"), lax.axis_index("ga"), lax.axis_index("sub")
    depth, half = eig.shape
    rows = exch.shape[1]
    part = rows // 2
    chunks = eig_sem.shape[0]
    width = depth // chunks
    groups = n * n_ga
    rank = z * n_ga + x
    pieced = len(dens.shape) == 3

    def cols(k):
        return slice(None) if chunks == 1 else span(k * width, width, 128)

    def eig_copy(k):
        at = span(k * width, width, 16)
        return pltpu.make_async_copy(basis.at[0, at], eig.at[at], eig_sem.at[k])

    def own_copy():
        src = dens.at[z] if pieced else dens.at[:, span(z * depth, depth, 128)]
        return pltpu.make_async_copy(src, exch.at[z], own_sem)

    mine = span(c * part, part, part)

    def sending(k, d):
        to = flipped(z, d)
        if pieced:
            src = dens.at[to, mine]
        else:
            src = dens.at[mine, span(to * depth + k * width, width, 128)]
        return pltpu.make_async_remote_copy(
            src_ref=src, dst_ref=exch.at[z, mine, cols(k)],
            send_sem=send.at[k, d - 1], recv_sem=recv.at[k, d - 1],
            device_id={"pair": to}, device_id_type=MESH)

    def forwarding(k, d):
        here = exch.at[flipped(z, d), mine, cols(k)]
        return pltpu.make_async_remote_copy(
            src_ref=here, dst_ref=here,
            send_sem=fwd_send.at[k, d - 1], recv_sem=fwd_recv.at[k, d - 1],
            device_id={"sub": 1 - c}, device_id_type=MESH)

    def peer(e):
        to = flipped(rank, e)
        return to, {"pair": to // n_ga, "ga": to % n_ga}

    def loop(count, body):
        lax.fori_loop(0, count, lambda i, _: (body(i), 0)[1], 0)

    loop(chunks, lambda k: eig_copy(k).start())
    own_copy().start()

    barrier = pltpu.get_barrier_semaphore()
    greeted = range(n_ga, groups, n_ga)
    for e in greeted:
        pl.semaphore_signal(barrier, inc=1, device_id=peer(e)[1], device_id_type=MESH)
    pl.semaphore_signal(barrier, inc=1, device_id={"sub": 1 - c}, device_id_type=MESH)
    pl.semaphore_wait(barrier, len(greeted) + 1)

    far_first = range(n - 1, 0, -1)

    def send_chunk(k):
        for d in far_first:
            sending(k, d).start()

    loop(chunks, send_chunk)
    total[...] = jnp.zeros_like(total)
    own_copy().wait()

    def step(k):
        @pl.when(k < chunks)
        def _():
            for d in far_first:
                sending(k, d).wait_recv()
                forwarding(k, d).start()

        @pl.when(k > 0)
        def _():
            last = k - 1
            eig_copy(last).wait()
            for d in far_first:
                forwarding(last, d).wait_recv()
            left = exch[:, :, cols(last)].reshape(n * rows, width)

            def tile(j):
                at = span(j * TILE, TILE, TILE)
                total[:, at] += jnp.dot(
                    left, eig[span(last * width, width, 16), at],
                    preferred_element_type=jnp.float32)

            loop(half // TILE, tile)

    loop(chunks + 1, step)

    def drain(k):
        for d in far_first:
            sending(k, d).wait_send()
            forwarding(k, d).wait_send()

    loop(chunks, drain)


def fused_kernel(
    n, n_ga, chunks, dens, basis, coef_out, block_out, eig, exch, total, x_in, z_in, coef, other,
    eig_sem, own_sem, send, recv, fwd_send, fwd_recv,
    x_send, x_recv, z_send, z_recv, all_send, all_recv, sib_send, sib_recv,
):
    z, x, c = lax.axis_index("pair"), lax.axis_index("ga"), lax.axis_index("sub")
    depth, half = eig.shape
    _, stages, part, _ = coef.shape
    reach = depth // 2
    width = reach // chunks
    steps = stages * chunks
    groups = n * n_ga
    rank = z * n_ga + x
    share = n // n_ga
    strip = half // n
    far_first = range(n - 1, 0, -1)

    def eig_copy(k, h):
        at = span(h * reach + k * width, width, 256)
        return pltpu.make_async_copy(basis.at[0, at], eig.at[at], eig_sem.at[k, h])

    def own_copy():
        return pltpu.make_async_copy(dens.at[:, span(z * depth, depth, 256)], exch.at[z], own_sem)

    def piece(g):
        s, k = divmod(g, chunks)
        return pl.ds(s * part, part), c * reach + k * width

    def sending(g, d):
        to = flipped(z, d)
        rows, at = piece(g)
        return pltpu.make_async_remote_copy(
            src_ref=dens.at[rows, span(to * depth + at, width, 256)],
            dst_ref=exch.at[z, rows, span(at, width, 256)],
            send_sem=send.at[g, d - 1], recv_sem=recv.at[g, d - 1],
            device_id={"pair": to}, device_id_type=MESH)

    def forwarding(g, d):
        rows, at = piece(g)
        here = exch.at[flipped(z, d), rows, span(at, width, 256)]
        return pltpu.make_async_remote_copy(
            src_ref=here, dst_ref=here,
            send_sem=fwd_send.at[g, d - 1], recv_sem=fwd_recv.at[g, d - 1],
            device_id={"sub": 1 - c}, device_id_type=MESH)

    def peer(e):
        to = flipped(rank, e)
        return {"pair": to // n_ga, "ga": to % n_ga}

    def kept(to):
        return pl.ds(to * share, share)

    def strip_of(to):
        return span(to * strip, strip, strip)

    def x_sum(s, e):
        to = flipped(x, e)
        return pltpu.make_async_remote_copy(
            src_ref=total.at[s, kept(to)], dst_ref=x_in.at[s, e - 1],
            send_sem=x_send.at[s, e - 1], recv_sem=x_recv.at[s, e - 1],
            device_id={"ga": to}, device_id_type=MESH)

    def z_sum(s, d):
        to = flipped(z, d)
        return pltpu.make_async_remote_copy(
            src_ref=total.at[s, kept(x), :, strip_of(to)], dst_ref=z_in.at[s, d - 1],
            send_sem=z_send.at[s, d - 1], recv_sem=z_recv.at[s, d - 1],
            device_id={"pair": to}, device_id_type=MESH)

    def sharing(s, e):
        here = coef.at[kept(x), s, :, strip_of(z)]
        return pltpu.make_async_remote_copy(
            src_ref=here, dst_ref=here,
            send_sem=all_send.at[s, e - 1], recv_sem=all_recv.at[s, e - 1],
            device_id=peer(e), device_id_type=MESH)

    def begin_x(s):
        for e in range(1, n_ga):
            x_sum(s, e).start()

    def begin_z(s):
        acc = total[s, kept(x)]
        for e in range(1, n_ga):
            x_sum(s, e).wait_recv()
            acc = acc + x_in[s, e - 1]
        total[s, kept(x)] = acc
        for d in far_first:
            z_sum(s, d).start()

    def begin_sharing(s):
        acc = total[s, kept(x), :, strip_of(z)]
        for d in far_first:
            z_sum(s, d).wait_recv()
            acc = acc + z_in[s, d - 1]
        coef[kept(x), s, :, strip_of(z)] = acc.astype(jnp.bfloat16)
        for e in range(groups - 1, 0, -1):
            sharing(s, e).start()

    def multiply(g):
        s, k = divmod(g, chunks)
        if s == 0:
            for h in range(2):
                eig_copy(k, h).wait()
        for d in far_first:
            forwarding(g, d).wait_recv()

        def tile(j, carry):
            at = span(j * TILE, TILE, TILE)
            acc = 0.0
            for h in range(2):
                deep = pl.ds(h * reach + k * width, width)
                left = exch[:, pl.ds(s * part, part), deep].reshape(n * part, width)
                acc += jnp.dot(left, eig[deep, at], preferred_element_type=jnp.float32)
            acc = acc.reshape(n, part, TILE)
            if k:
                acc += total[s, :, :, at]
            total[s, :, :, at] = acc
            return carry

        lax.fori_loop(0, half // TILE, tile, 0)

    for k in range(chunks):
        for h in range(2):
            eig_copy(k, h).start()
    own_copy().start()

    barrier = pltpu.get_barrier_semaphore()
    for e in range(1, groups):
        pl.semaphore_signal(barrier, inc=1, device_id=peer(e), device_id_type=MESH)
    pl.semaphore_signal(barrier, inc=1, device_id={"sub": 1 - c}, device_id_type=MESH)
    pl.semaphore_wait(barrier, groups)

    for g in range(min(AHEAD, steps)):
        for d in far_first:
            sending(g, d).start()
    own_copy().wait()

    after = {}
    for s in range(stages - 1):
        done = (s + 1) * chunks
        gap = max(1, (chunks - 1) // 2)
        after.setdefault(done, []).append((begin_x, s))
        after.setdefault(done + gap, []).append((begin_z, s))
        after.setdefault(done + 2 * gap, []).append((begin_sharing, s))

    for g in range(steps + 1):
        if g < steps:
            for d in far_first:
                sending(g, d).wait_recv()
                forwarding(g, d).start()
            if g + AHEAD < steps:
                for d in far_first:
                    sending(g + AHEAD, d).start()
        if g > 0:
            multiply(g - 1)
        for act, s in after.get(g, []):
            act(s)

    last = stages - 1
    begin_x(last)
    for g in range(steps):
        for d in far_first:
            sending(g, d).wait_send()
            forwarding(g, d).wait_send()
    begin_z(last)
    begin_sharing(last)
    for s in range(stages):
        for e in range(1, n_ga):
            x_sum(s, e).wait_send()
        for d in far_first:
            z_sum(s, d).wait_send()
    for s in range(stages):
        for e in range(1, groups):
            sharing(s, e).wait()

    block = 2 * half // groups
    per_half = groups // 2
    at = span((rank % per_half) * block, block, block)
    sibling = pltpu.make_async_remote_copy(
        src_ref=coef.at[:, :, :, at], dst_ref=other, send_sem=sib_send, recv_sem=sib_recv,
        device_id={"sub": 1 - c}, device_id_type=MESH)
    sibling.start()
    coef_out[...] = coef[...]
    sibling.wait()
    here = rank // per_half == c

    @pl.when(here)
    def _():
        block_out[...] = coef[:, :, :, at]

    @pl.when(jnp.logical_not(here))
    def _():
        block_out[...] = other[...]


def final_kernel(scale, coef, columns, energies, frequencies, out, turned):
    w = pl.program_id(0)

    @pl.when(w == 0)
    def _():
        turned[...] = coef[...].T

    pairs, width = columns.shape
    energy = jnp.broadcast_to(energies[...], (128, pairs)).T
    frequency = frequencies[w]
    factor = 2.0 * energy / (energy * energy + frequency * frequency)
    for i in range(0, width, 128):
        weighted = (factor * columns[:, i:i + 128].astype(jnp.float32)).astype(jnp.bfloat16)
        if i % 256 == 0:
            held = [weighted]
        else:
            held.append(weighted)
        if i % 256 == 128 or i + 128 == width:
            start = i + 128 - 128 * len(held)
            right = jnp.concatenate(held, axis=1)
            value = jnp.dot(turned[...], right, preferred_element_type=jnp.float32)
            out[0, :, start:i + 128] = value * scale


def plain(densities, eigvecs, n, n_ga):
    rows = densities.shape[0]
    _, depth, half = eigvecs.shape
    chunks = depth // WIDTH if depth % WIDTH == 0 else 1
    if depth % 128:
        densities = densities.reshape(rows, n, depth).transpose(1, 0, 2)
    dma = pltpu.SemaphoreType.DMA
    any_space = pl.BlockSpec(memory_space=pl.ANY)
    return pl.pallas_call(
        functools.partial(plain_kernel, n, n_ga),
        out_shape=jax.ShapeDtypeStruct((n * rows, half), jnp.float32),
        in_specs=[any_space, any_space],
        out_specs=pl.BlockSpec(memory_space=pltpu.VMEM),
        scratch_shapes=[
            pltpu.VMEM((depth, half), jnp.bfloat16),
            pltpu.VMEM((n, rows, depth), jnp.bfloat16),
            dma((chunks,)), dma,
        ] + [dma((chunks, n - 1))] * 4,
        compiler_params=pltpu.CompilerParams(
            collective_id=0, has_side_effects=True, vmem_limit_bytes=56 * 1024 * 1024),
    )(densities, eigvecs)


def fused(densities, eigvecs, n, n_ga):
    rows = densities.shape[0]
    _, depth, half = eigvecs.shape
    groups = n * n_ga
    chunks = depth // (2 * WIDTH)
    part, block, share = rows // STAGES, 2 * half // groups, n // n_ga
    dma = pltpu.SemaphoreType.DMA
    any_space = pl.BlockSpec(memory_space=pl.ANY)
    vmem = pl.BlockSpec(memory_space=pltpu.VMEM)
    coef_shape, block_shape = (n, STAGES, part, half), (n, STAGES, part, block)
    coef, columns = pl.pallas_call(
        functools.partial(fused_kernel, n, n_ga, chunks),
        out_shape=(
            jax.ShapeDtypeStruct(coef_shape, jnp.bfloat16),
            jax.ShapeDtypeStruct(block_shape, jnp.bfloat16),
        ),
        in_specs=[any_space, any_space],
        out_specs=(vmem, vmem),
        scratch_shapes=[
            pltpu.VMEM((depth, half), jnp.bfloat16),
            pltpu.VMEM((n, rows, depth), jnp.bfloat16),
            pltpu.VMEM((STAGES, n, part, half), jnp.float32),
            pltpu.VMEM((STAGES, n_ga - 1, share, part, half), jnp.float32),
            pltpu.VMEM((STAGES, n - 1, share, part, half // n), jnp.float32),
            pltpu.VMEM(coef_shape, jnp.bfloat16),
            pltpu.VMEM(block_shape, jnp.bfloat16),
            dma((chunks, 2)), dma,
        ] + [dma((STAGES * chunks, n - 1))] * 4 + [
            dma((STAGES, n_ga - 1)), dma((STAGES, n_ga - 1)),
            dma((STAGES, n - 1)), dma((STAGES, n - 1)),
            dma((STAGES, groups - 1)), dma((STAGES, groups - 1)), dma, dma,
        ],
        compiler_params=pltpu.CompilerParams(
            collective_id=0, has_side_effects=True, vmem_limit_bytes=56 * 1024 * 1024),
        cost_estimate=pl.CostEstimate(
            flops=2 * n * rows * depth * half, transcendentals=0,
            bytes_accessed=2 * depth * (half + n * rows)),
    )(densities, eigvecs)
    return coef.reshape(n * rows, half), columns.reshape(n * rows, block)


def final(coef, columns, energies, frequencies):
    pairs, half = coef.shape
    block = columns.shape[1]
    count = frequencies.shape[0]
    return pl.pallas_call(
        functools.partial(final_kernel, -1.0 / pairs),
        grid=(count,),
        out_shape=jax.ShapeDtypeStruct((count, half, block), jnp.float32),
        in_specs=[
            pl.BlockSpec((pairs, half), lambda w: (0, 0)),
            pl.BlockSpec((pairs, block), lambda w: (0, 0)),
            pl.BlockSpec((1, pairs), lambda w: (0, 0)),
            pl.BlockSpec(memory_space=pltpu.SMEM),
        ],
        out_specs=pl.BlockSpec((1, half, block), lambda w: (w, 0, 0)),
        scratch_shapes=[pltpu.VMEM((half, pairs), jnp.bfloat16)],
        compiler_params=pltpu.CompilerParams(vmem_limit_bytes=16 * 1024 * 1024),
    )(coef, columns, energies.reshape(1, pairs), frequencies)


def on_device(densities, eigvecs, energies, frequencies):
    n, n_ga = lax.axis_size("pair"), lax.axis_size("ga")
    rows, depth, half = densities.shape[0], eigvecs.shape[1], eigvecs.shape[2]
    groups = n * n_ga
    fits = (
        depth % (2 * WIDTH) == 0 and rows % (16 * STAGES) == 0 and n % n_ga == 0
        and half % (128 * n) == 0 and (2 * half) % (128 * groups) == 0 and groups % 2 == 0
    )
    if fits:
        coefficients, columns = fused(densities, eigvecs, n, n_ga)
        return final(coefficients, columns, energies, frequencies)
    partial_value = plain(densities, eigvecs, n, n_ga)
    coefficients = lax.psum(partial_value, ("pair", "ga")).astype(jnp.bfloat16)
    width = 2 * half // groups
    start = (lax.axis_index("pair") * n_ga + lax.axis_index("ga")) * width
    swapped = lax.ppermute(coefficients, "sub", [(0, 1), (1, 0)])
    first = lax.axis_index("sub") == 0
    whole = jnp.concatenate(
        [jnp.where(first, coefficients, swapped), jnp.where(first, swapped, coefficients)], axis=1)
    columns = lax.dynamic_slice_in_dim(whole, start, width, 1)
    squared = energies * energies
    factor = (
        2.0 * energies[None, :] / (squared[None, :] + frequencies[:, None] * frequencies[:, None])
    )
    weighted = (factor[:, :, None] * columns.astype(jnp.float32)[None, :, :]).astype(jnp.bfloat16)
    result = jnp.einsum("ps,wpt->wst", coefficients, weighted, preferred_element_type=jnp.float32)
    return result * (-1.0 / (n * rows))


def solution(mesh):
    placed = (P(("grp", "pair"), "ga"), P("ga", "pair", "sub"), P("grp"), P())
    return jax.shard_map(
        on_device,
        mesh=mesh,
        in_specs=placed,
        out_specs=P("grp", "sub", ("pair", "ga")),
        check_vma=False,
    )
```

```python
import functools

import jax
import jax.numpy as jnp
from jax import lax
from jax.experimental import pallas as pl
from jax.experimental.pallas import tpu as pltpu
from jax.sharding import PartitionSpec as P

MESH = pl.DeviceIdType.MESH
WIDTH = 1536
TILE = 256
STAGES = 2
AHEAD = 4


def flipped(index, bits):
    bit = 1
    while bit <= bits:
        if bits & bit:
            index = index + bit - 2 * bit * ((index // bit) % 2)
        bit *= 2
    return index


def span(start, size, unit):
    return pl.ds(pl.multiple_of(start, unit), size)


def plain_kernel(n, n_ga, dens, basis, total, eig, exch, eig_sem, own_sem, send, recv, fwd_send, fwd_recv):
    z, x, c = lax.axis_index("pair"), lax.axis_index("ga"), lax.axis_index("sub")
    depth, half = eig.shape
    rows = exch.shape[1]
    part = rows // 2
    chunks = eig_sem.shape[0]
    width = depth // chunks
    groups = n * n_ga
    rank = z * n_ga + x
    pieced = len(dens.shape) == 3

    def cols(k):
        return slice(None) if chunks == 1 else span(k * width, width, 128)

    def eig_copy(k):
        at = span(k * width, width, 16)
        return pltpu.make_async_copy(basis.at[0, at], eig.at[at], eig_sem.at[k])

    def own_copy():
        src = dens.at[z] if pieced else dens.at[:, span(z * depth, depth, 128)]
        return pltpu.make_async_copy(src, exch.at[z], own_sem)

    mine = span(c * part, part, part)

    def sending(k, d):
        to = flipped(z, d)
        if pieced:
            src = dens.at[to, mine]
        else:
            src = dens.at[mine, span(to * depth + k * width, width, 128)]
        return pltpu.make_async_remote_copy(
            src_ref=src, dst_ref=exch.at[z, mine, cols(k)],
            send_sem=send.at[k, d - 1], recv_sem=recv.at[k, d - 1],
            device_id={"pair": to}, device_id_type=MESH)

    def forwarding(k, d):
        here = exch.at[flipped(z, d), mine, cols(k)]
        return pltpu.make_async_remote_copy(
            src_ref=here, dst_ref=here,
            send_sem=fwd_send.at[k, d - 1], recv_sem=fwd_recv.at[k, d - 1],
            device_id={"sub": 1 - c}, device_id_type=MESH)

    def peer(e):
        to = flipped(rank, e)
        return to, {"pair": to // n_ga, "ga": to % n_ga}

    def loop(count, body):
        lax.fori_loop(0, count, lambda i, _: (body(i), 0)[1], 0)

    loop(chunks, lambda k: eig_copy(k).start())
    own_copy().start()

    barrier = pltpu.get_barrier_semaphore()
    greeted = range(n_ga, groups, n_ga)
    for e in greeted:
        pl.semaphore_signal(barrier, inc=1, device_id=peer(e)[1], device_id_type=MESH)
    pl.semaphore_signal(barrier, inc=1, device_id={"sub": 1 - c}, device_id_type=MESH)
    pl.semaphore_wait(barrier, len(greeted) + 1)

    far_first = range(n - 1, 0, -1)

    def send_chunk(k):
        for d in far_first:
            sending(k, d).start()

    loop(chunks, send_chunk)
    total[...] = jnp.zeros_like(total)
    own_copy().wait()

    def step(k):
        @pl.when(k < chunks)
        def _():
            for d in far_first:
                sending(k, d).wait_recv()
                forwarding(k, d).start()

        @pl.when(k > 0)
        def _():
            last = k - 1
            eig_copy(last).wait()
            for d in far_first:
                forwarding(last, d).wait_recv()
            left = exch[:, :, cols(last)].reshape(n * rows, width)

            def tile(j):
                at = span(j * TILE, TILE, TILE)
                total[:, at] += jnp.dot(
                    left, eig[span(last * width, width, 16), at],
                    preferred_element_type=jnp.float32)

            loop(half // TILE, tile)

    loop(chunks + 1, step)

    def drain(k):
        for d in far_first:
            sending(k, d).wait_send()
            forwarding(k, d).wait_send()

    loop(chunks, drain)


def fused_kernel(
    n, n_ga, chunks, dens, basis, coef_out, block_out, eig, exch, total, x_in, z_in, coef, other,
    eig_sem, own_sem, send, recv, fwd_send, fwd_recv,
    x_send, x_recv, z_send, z_recv, all_send, all_recv, sib_send, sib_recv,
):
    z, x, c = lax.axis_index("pair"), lax.axis_index("ga"), lax.axis_index("sub")
    depth, half = eig.shape
    _, stages, part, _ = coef.shape
    reach = depth // 2
    width = reach // chunks
    steps = stages * chunks
    groups = n * n_ga
    rank = z * n_ga + x
    share = n // n_ga
    strip = half // n
    far_first = range(n - 1, 0, -1)
    all_far_first = range(n - 1, -1, -1)
    crosses = (rank // n + c) % 2

    def eig_copy(k, h):
        at = span(h * reach + k * width, width, 256)
        return pltpu.make_async_copy(basis.at[0, at], eig.at[at], eig_sem.at[k, h])

    def own_copy():
        return pltpu.make_async_copy(dens.at[:, span(z * depth, depth, 256)], exch.at[z], own_sem)

    def piece(g):
        s, k = divmod(g, chunks)
        return pl.ds(s * part, part), c * reach + k * width

    def sending(g, d):
        to = flipped(z, d)
        rows, at = piece(g)
        return pltpu.make_async_remote_copy(
            src_ref=dens.at[rows, span(to * depth + at, width, 256)],
            dst_ref=exch.at[z, rows, span(at, width, 256)],
            send_sem=send.at[g, d - 1], recv_sem=recv.at[g, d - 1],
            device_id={"pair": to}, device_id_type=MESH)

    def forwarding(g, d):
        rows, at = piece(g)
        here = exch.at[flipped(z, d), rows, span(at, width, 256)]
        return pltpu.make_async_remote_copy(
            src_ref=here, dst_ref=here,
            send_sem=fwd_send.at[g, d - 1], recv_sem=fwd_recv.at[g, d - 1],
            device_id={"sub": 1 - c}, device_id_type=MESH)

    def peer(e):
        to = flipped(rank, e)
        return {"pair": to // n_ga, "ga": to % n_ga}

    def kept(to):
        return pl.ds(to * share, share)

    def strip_of(to):
        return span(to * strip, strip, strip)

    def x_sum(s, e, d):
        to, at = flipped(x, e), strip_of(flipped(z, d))
        return pltpu.make_async_remote_copy(
            src_ref=total.at[s, kept(to), :, at], dst_ref=x_in.at[s, e - 1, :, :, at],
            send_sem=x_send.at[s, e - 1, d], recv_sem=x_recv.at[s, e - 1, d],
            device_id={"ga": to}, device_id_type=MESH)

    def z_sum(s, d):
        to = flipped(z, d)
        return pltpu.make_async_remote_copy(
            src_ref=total.at[s, kept(x), :, strip_of(to)], dst_ref=z_in.at[s, d - 1],
            send_sem=z_send.at[s, d - 1], recv_sem=z_recv.at[s, d - 1],
            device_id={"pair": to}, device_id_type=MESH)

    def sharing(s, e):
        here = coef.at[kept(x), s, :, strip_of(z)]
        return pltpu.make_async_remote_copy(
            src_ref=here, dst_ref=here,
            send_sem=all_send.at[s, e - 1], recv_sem=all_recv.at[s, e - 1],
            device_id=peer(e), device_id_type=MESH)

    def crossing(s):
        to = c * n + z
        return pltpu.make_async_remote_copy(
            src_ref=coef.at[kept(x), s, :, strip_of(z)], dst_ref=other.at[kept(x), s],
            send_sem=sib_send.at[s], recv_sem=sib_recv.at[s, x],
            device_id={"pair": to // n_ga, "ga": to % n_ga, "sub": 1 - c}, device_id_type=MESH)

    def crossed(s, e):
        here = other.at[pl.ds(e * share, share), s]
        return pltpu.make_async_remote_copy(
            src_ref=here, dst_ref=here, send_sem=sib_send.at[s], recv_sem=sib_recv.at[s, e],
            device_id={"sub": 1 - c}, device_id_type=MESH)

    def begin_x(s):
        for d in all_far_first:
            for e in range(1, n_ga):
                x_sum(s, e, d).start()

    def begin_z(s):
        for d in all_far_first:
            at = strip_of(flipped(z, d))
            acc = total[s, kept(x), :, at]
            for e in range(1, n_ga):
                x_sum(s, e, d).wait_recv()
                acc = acc + x_in[s, e - 1, :, :, at]
            total[s, kept(x), :, at] = acc
            if d:
                z_sum(s, d).start()

    def begin_sharing(s):
        acc = total[s, kept(x), :, strip_of(z)]
        for d in far_first:
            z_sum(s, d).wait_recv()
            acc = acc + z_in[s, d - 1]
        coef[kept(x), s, :, strip_of(z)] = acc.astype(jnp.bfloat16)
        for e in range(groups - 1, 0, -1):
            sharing(s, e).start()
        crossing(s).start()

    def multiply(g):
        s, k = divmod(g, chunks)
        if s == 0:
            for h in range(2):
                eig_copy(k, h).wait()
        for d in far_first:
            forwarding(g, d).wait_recv()

        def tile(j, carry):
            at = strip_of(j)
            acc = 0.0
            for h in range(2):
                deep = pl.ds(h * reach + k * width, width)
                left = exch[:, pl.ds(s * part, part), deep].reshape(n * part, width)
                acc += jnp.dot(left, eig[deep, at], preferred_element_type=jnp.float32)
            acc = acc.reshape(n, part, strip)
            if k:
                acc += total[s, :, :, at]
            total[s, :, :, at] = acc
            return carry

        if g < steps - 1:
            lax.fori_loop(0, n, tile, 0)
        else:
            for d in all_far_first:
                tile(flipped(z, d), 0)
                for e in range(1, n_ga):
                    x_sum(s, e, d).start()

    for k in range(chunks):
        for h in range(2):
            eig_copy(k, h).start()
    own_copy().start()

    barrier = pltpu.get_barrier_semaphore()
    for e in range(1, groups):
        pl.semaphore_signal(barrier, inc=1, device_id=peer(e), device_id_type=MESH)
    pl.semaphore_signal(barrier, inc=1, device_id={"sub": 1 - c}, device_id_type=MESH)
    pl.semaphore_signal(
        barrier, inc=1, device_id_type=MESH,
        device_id={"pair": (c * n + z) // n_ga, "ga": (c * n + z) % n_ga, "sub": 1 - c})

    @pl.when(crosses == 1)
    def _():
        for e in range(n_ga):
            pl.semaphore_signal(
                barrier, inc=1, device_id={"pair": rank % n, "ga": e, "sub": 1 - c},
                device_id_type=MESH)

    pl.semaphore_wait(barrier, groups + 1 + n_ga * crosses)

    for g in range(min(AHEAD, steps)):
        for d in far_first:
            sending(g, d).start()
    own_copy().wait()

    after = {}
    for s in range(stages - 1):
        done = (s + 1) * chunks
        gap = max(1, (chunks - 1) // 2)
        after.setdefault(done, []).append((begin_x, s))
        after.setdefault(done + gap, []).append((begin_z, s))
        after.setdefault(done + 2 * gap, []).append((begin_sharing, s))

    for g in range(steps + 1):
        if g < steps:
            for d in far_first:
                sending(g, d).wait_recv()
                forwarding(g, d).start()
            if g + AHEAD < steps:
                for d in far_first:
                    sending(g + AHEAD, d).start()
        if g > 0:
            multiply(g - 1)
        for act, s in after.get(g, []):
            act(s)

    last = stages - 1
    begin_z(last)
    for g in range(steps):
        for d in far_first:
            sending(g, d).wait_send()
            forwarding(g, d).wait_send()
    begin_sharing(last)
    for s in range(stages):
        for e in range(1, n_ga):
            for d in all_far_first:
                x_sum(s, e, d).wait_send()
        for d in far_first:
            z_sum(s, d).wait_send()
    for s in range(stages):
        for e in range(1, groups):
            sharing(s, e).wait()

    coef_out[...] = coef[...]
    for s in range(stages):
        crossing(s).wait_send()

    @pl.when(crosses == 0)
    def _():
        block_out[...] = coef[:, :, :, strip_of(rank % n)]

    @pl.when(crosses == 1)
    def _():
        for s in range(stages):
            for e in range(n_ga):
                crossed(s, e).wait_recv()
        block_out[...] = other[...]


def final_kernel(scale, coef, columns, energies, frequencies, out, held, done):
    count, half, width = held.shape
    pairs = coef.shape[0]
    turned = coef[...].T
    energy = jnp.broadcast_to(energies[...], (128, pairs)).T
    squared = energy * energy
    wide = columns[...].astype(jnp.float32)

    def copy(w):
        return pltpu.make_async_copy(held.at[w], out.at[w], done.at[w])

    for w in range(count):
        frequency = frequencies[w]
        factor = 2.0 * energy / (squared + frequency * frequency)
        weighted = [factor * wide[:, i:i + 128] for i in range(0, width, 128)]
        right = jnp.concatenate(weighted, axis=1).astype(jnp.bfloat16)
        held[w] = jnp.dot(turned, right, preferred_element_type=jnp.float32) * scale
        copy(w).start()
    for w in range(count):
        copy(w).wait()


def plain(densities, eigvecs, n, n_ga):
    rows = densities.shape[0]
    _, depth, half = eigvecs.shape
    chunks = depth // WIDTH if depth % WIDTH == 0 else 1
    if depth % 128:
        densities = densities.reshape(rows, n, depth).transpose(1, 0, 2)
    dma = pltpu.SemaphoreType.DMA
    any_space = pl.BlockSpec(memory_space=pl.ANY)
    return pl.pallas_call(
        functools.partial(plain_kernel, n, n_ga),
        out_shape=jax.ShapeDtypeStruct((n * rows, half), jnp.float32),
        in_specs=[any_space, any_space],
        out_specs=pl.BlockSpec(memory_space=pltpu.VMEM),
        scratch_shapes=[
            pltpu.VMEM((depth, half), jnp.bfloat16),
            pltpu.VMEM((n, rows, depth), jnp.bfloat16),
            dma((chunks,)), dma,
        ] + [dma((chunks, n - 1))] * 4,
        compiler_params=pltpu.CompilerParams(
            collective_id=0, has_side_effects=True, vmem_limit_bytes=56 * 1024 * 1024),
    )(densities, eigvecs)


def fused(densities, eigvecs, n, n_ga):
    rows = densities.shape[0]
    _, depth, half = eigvecs.shape
    groups = n * n_ga
    chunks = depth // (2 * WIDTH)
    part, block, share = rows // STAGES, 2 * half // groups, n // n_ga
    dma = pltpu.SemaphoreType.DMA
    any_space = pl.BlockSpec(memory_space=pl.ANY)
    vmem = pl.BlockSpec(memory_space=pltpu.VMEM)
    coef_shape, block_shape = (n, STAGES, part, half), (n, STAGES, part, block)
    coef, columns = pl.pallas_call(
        functools.partial(fused_kernel, n, n_ga, chunks),
        out_shape=(
            jax.ShapeDtypeStruct(coef_shape, jnp.bfloat16),
            jax.ShapeDtypeStruct(block_shape, jnp.bfloat16),
        ),
        in_specs=[any_space, any_space],
        out_specs=(vmem, vmem),
        scratch_shapes=[
            pltpu.VMEM((depth, half), jnp.bfloat16),
            pltpu.VMEM((n, rows, depth), jnp.bfloat16),
            pltpu.VMEM((STAGES, n, part, half), jnp.float32),
            pltpu.VMEM((STAGES, n_ga - 1, share, part, half), jnp.float32),
            pltpu.VMEM((STAGES, n - 1, share, part, half // n), jnp.float32),
            pltpu.VMEM(coef_shape, jnp.bfloat16),
            pltpu.VMEM(block_shape, jnp.bfloat16),
            dma((chunks, 2)), dma,
        ] + [dma((STAGES * chunks, n - 1))] * 4 + [
            dma((STAGES, n_ga - 1, n)), dma((STAGES, n_ga - 1, n)),
            dma((STAGES, n - 1)), dma((STAGES, n - 1)),
            dma((STAGES, groups - 1)), dma((STAGES, groups - 1)),
            dma((STAGES,)), dma((STAGES, n_ga)),
        ],
        compiler_params=pltpu.CompilerParams(
            collective_id=0, has_side_effects=True, vmem_limit_bytes=56 * 1024 * 1024),
        cost_estimate=pl.CostEstimate(
            flops=2 * n * rows * depth * half, transcendentals=0,
            bytes_accessed=2 * depth * (half + n * rows)),
    )(densities, eigvecs)
    return coef.reshape(n * rows, half), columns.reshape(n * rows, block)


def final(coef, columns, energies, frequencies):
    pairs, half = coef.shape
    block = columns.shape[1]
    count = frequencies.shape[0]
    vmem = pl.BlockSpec(memory_space=pltpu.VMEM)
    return pl.pallas_call(
        functools.partial(final_kernel, -1.0 / pairs),
        out_shape=jax.ShapeDtypeStruct((count, half, block), jnp.float32),
        in_specs=[vmem, vmem, vmem, pl.BlockSpec(memory_space=pltpu.SMEM)],
        out_specs=pl.BlockSpec(memory_space=pl.ANY),
        scratch_shapes=[
            pltpu.VMEM((count, half, block), jnp.float32), pltpu.SemaphoreType.DMA((count,)),
        ],
        compiler_params=pltpu.CompilerParams(vmem_limit_bytes=16 * 1024 * 1024),
    )(coef, columns, energies.reshape(1, pairs), frequencies)


def on_device(densities, eigvecs, energies, frequencies):
    n, n_ga = lax.axis_size("pair"), lax.axis_size("ga")
    rows, depth, half = densities.shape[0], eigvecs.shape[1], eigvecs.shape[2]
    groups = n * n_ga
    fits = (
        depth % (2 * WIDTH) == 0 and rows % (16 * STAGES) == 0 and n % n_ga == 0
        and half % (128 * n) == 0 and n_ga == 2
    )
    if fits:
        coefficients, columns = fused(densities, eigvecs, n, n_ga)
        return final(coefficients, columns, energies, frequencies)
    partial_value = plain(densities, eigvecs, n, n_ga)
    coefficients = lax.psum(partial_value, ("pair", "ga")).astype(jnp.bfloat16)
    width = 2 * half // groups
    start = (lax.axis_index("pair") * n_ga + lax.axis_index("ga")) * width
    swapped = lax.ppermute(coefficients, "sub", [(0, 1), (1, 0)])
    first = lax.axis_index("sub") == 0
    whole = jnp.concatenate(
        [jnp.where(first, coefficients, swapped), jnp.where(first, swapped, coefficients)], axis=1)
    columns = lax.dynamic_slice_in_dim(whole, start, width, 1)
    squared = energies * energies
    factor = (
        2.0 * energies[None, :] / (squared[None, :] + frequencies[:, None] * frequencies[:, None])
    )
    weighted = (factor[:, :, None] * columns.astype(jnp.float32)[None, :, :]).astype(jnp.bfloat16)
    result = jnp.einsum("ps,wpt->wst", coefficients, weighted, preferred_element_type=jnp.float32)
    return result * (-1.0 / (n * rows))


def solution(mesh):
    placed = (P(("grp", "pair"), "ga"), P("ga", "pair", "sub"), P("grp"), P())
    return jax.shard_map(
        on_device,
        mesh=mesh,
        in_specs=placed,
        out_specs=P("grp", "sub", ("pair", "ga")),
        check_vma=False,
    )
```

```python
import functools

import jax
import jax.numpy as jnp
from jax import lax
from jax.experimental import pallas as pl
from jax.experimental.pallas import tpu as pltpu
from jax.sharding import PartitionSpec as P

MESH = pl.DeviceIdType.MESH
WIDTH = 2560
LAST_WIDTHS = (1536, 1024)
RELAYED = (False, False)
TILE = 256
STAGES = 2
AHEAD = 4


def flipped(index, bits):
    bit = 1
    while bit <= bits:
        if bits & bit:
            index = index + bit - 2 * bit * ((index // bit) % 2)
        bit *= 2
    return index


def span(start, size, unit):
    return pl.ds(pl.multiple_of(start, unit), size)


def plain_kernel(n, n_ga, dens, basis, total, eig, exch, eig_sem, own_sem, send, recv, fwd_send, fwd_recv):
    z, x, c = lax.axis_index("pair"), lax.axis_index("ga"), lax.axis_index("sub")
    depth, half = eig.shape
    rows = exch.shape[1]
    part = rows // 2
    chunks = eig_sem.shape[0]
    width = depth // chunks
    groups = n * n_ga
    rank = z * n_ga + x
    pieced = len(dens.shape) == 3

    def cols(k):
        return slice(None) if chunks == 1 else span(k * width, width, 128)

    def eig_copy(k):
        at = span(k * width, width, 16)
        return pltpu.make_async_copy(basis.at[0, at], eig.at[at], eig_sem.at[k])

    def own_copy():
        src = dens.at[z] if pieced else dens.at[:, span(z * depth, depth, 128)]
        return pltpu.make_async_copy(src, exch.at[z], own_sem)

    mine = span(c * part, part, part)

    def sending(k, d):
        to = flipped(z, d)
        if pieced:
            src = dens.at[to, mine]
        else:
            src = dens.at[mine, span(to * depth + k * width, width, 128)]
        return pltpu.make_async_remote_copy(
            src_ref=src, dst_ref=exch.at[z, mine, cols(k)],
            send_sem=send.at[k, d - 1], recv_sem=recv.at[k, d - 1],
            device_id={"pair": to}, device_id_type=MESH)

    def forwarding(k, d):
        here = exch.at[flipped(z, d), mine, cols(k)]
        return pltpu.make_async_remote_copy(
            src_ref=here, dst_ref=here,
            send_sem=fwd_send.at[k, d - 1], recv_sem=fwd_recv.at[k, d - 1],
            device_id={"sub": 1 - c}, device_id_type=MESH)

    def peer(e):
        to = flipped(rank, e)
        return to, {"pair": to // n_ga, "ga": to % n_ga}

    def loop(count, body):
        lax.fori_loop(0, count, lambda i, _: (body(i), 0)[1], 0)

    loop(chunks, lambda k: eig_copy(k).start())
    own_copy().start()

    barrier = pltpu.get_barrier_semaphore()
    greeted = range(n_ga, groups, n_ga)
    for e in greeted:
        pl.semaphore_signal(barrier, inc=1, device_id=peer(e)[1], device_id_type=MESH)
    pl.semaphore_signal(barrier, inc=1, device_id={"sub": 1 - c}, device_id_type=MESH)
    pl.semaphore_wait(barrier, len(greeted) + 1)

    far_first = range(n - 1, 0, -1)

    def send_chunk(k):
        for d in far_first:
            sending(k, d).start()

    loop(chunks, send_chunk)
    total[...] = jnp.zeros_like(total)
    own_copy().wait()

    def step(k):
        @pl.when(k < chunks)
        def _():
            for d in far_first:
                sending(k, d).wait_recv()
                forwarding(k, d).start()

        @pl.when(k > 0)
        def _():
            last = k - 1
            eig_copy(last).wait()
            for d in far_first:
                forwarding(last, d).wait_recv()
            left = exch[:, :, cols(last)].reshape(n * rows, width)

            def tile(j):
                at = span(j * TILE, TILE, TILE)
                total[:, at] += jnp.dot(
                    left, eig[span(last * width, width, 16), at],
                    preferred_element_type=jnp.float32)

            loop(half // TILE, tile)

    loop(chunks + 1, step)

    def drain(k):
        for d in far_first:
            sending(k, d).wait_send()
            forwarding(k, d).wait_send()

    loop(chunks, drain)


def fused_kernel(
    n, n_ga, widths, dens, basis, coef_out, block_out, eig, exch, total, x_in, z_in, coef, other,
    eig_sem, own_sem, send, recv, fwd_send, fwd_recv,
    x_send, x_recv, z_send, z_recv, all_send, all_recv, sib_send, sib_recv,
):
    z, x, c = lax.axis_index("pair"), lax.axis_index("ga"), lax.axis_index("sub")
    depth, half = eig.shape
    _, stages, part, _ = coef.shape
    reach = depth // 2
    chunks = len(widths)
    starts = [sum(widths[:k]) for k in range(chunks)]
    steps = stages * chunks
    groups = n * n_ga
    rank = z * n_ga + x
    share = n // n_ga
    strip = half // n
    far_first = range(n - 1, 0, -1)
    all_far_first = range(n - 1, -1, -1)
    crosses = (rank // n + c) % 2

    def eig_copy(k, h):
        at = span(h * reach + starts[k], widths[k], 128)
        return pltpu.make_async_copy(basis.at[0, at], eig.at[at], eig_sem.at[k, h])

    def own_copy():
        return pltpu.make_async_copy(dens.at[:, span(z * depth, depth, 128)], exch.at[z], own_sem)

    def piece(g):
        s, k = divmod(g, chunks)
        return pl.ds(s * part, part), c * reach + starts[k], widths[k]

    def sending(g, d):
        to = flipped(z, d)
        rows, at, width = piece(g)
        return pltpu.make_async_remote_copy(
            src_ref=dens.at[rows, span(to * depth + at, width, 128)],
            dst_ref=exch.at[z, rows, span(at, width, 128)],
            send_sem=send.at[g, d - 1], recv_sem=recv.at[g, d - 1],
            device_id={"pair": to}, device_id_type=MESH)

    def forwarding(g, d):
        rows, at, width = piece(g)
        here = exch.at[flipped(z, d), rows, span(at, width, 128)]
        return pltpu.make_async_remote_copy(
            src_ref=here, dst_ref=here,
            send_sem=fwd_send.at[g, d - 1], recv_sem=fwd_recv.at[g, d - 1],
            device_id={"sub": 1 - c}, device_id_type=MESH)

    def peer(e):
        to = flipped(rank, e)
        return {"pair": to // n_ga, "ga": to % n_ga}

    def kept(to):
        return pl.ds(to * share, share)

    def strip_of(to):
        return span(to * strip, strip, strip)

    def x_sum(s, e, d):
        to, at = flipped(x, e), strip_of(flipped(z, d))
        return pltpu.make_async_remote_copy(
            src_ref=total.at[s, kept(to), :, at], dst_ref=x_in.at[s, e - 1, :, :, at],
            send_sem=x_send.at[s, e - 1, d], recv_sem=x_recv.at[s, e - 1, d],
            device_id={"ga": to}, device_id_type=MESH)

    def z_sum(s, d):
        to = flipped(z, d)
        return pltpu.make_async_remote_copy(
            src_ref=total.at[s, kept(x), :, strip_of(to)], dst_ref=z_in.at[s, d - 1],
            send_sem=z_send.at[s, d - 1], recv_sem=z_recv.at[s, d - 1],
            device_id={"pair": to}, device_id_type=MESH)

    def sharing(s, e):
        here = coef.at[kept(x), s, :, strip_of(z)]
        return pltpu.make_async_remote_copy(
            src_ref=here, dst_ref=here,
            send_sem=all_send.at[s, e - 1], recv_sem=all_recv.at[s, e - 1],
            device_id=peer(e), device_id_type=MESH)

    def crossing(s):
        to = c * n + z
        return pltpu.make_async_remote_copy(
            src_ref=coef.at[kept(x), s, :, strip_of(z)], dst_ref=other.at[kept(x), s],
            send_sem=sib_send.at[s], recv_sem=sib_recv.at[s, x],
            device_id={"pair": to // n_ga, "ga": to % n_ga, "sub": 1 - c}, device_id_type=MESH)

    def crossed(s, e):
        here = other.at[pl.ds(e * share, share), s]
        return pltpu.make_async_remote_copy(
            src_ref=here, dst_ref=here, send_sem=sib_send.at[s], recv_sem=sib_recv.at[s, e],
            device_id={"sub": 1 - c}, device_id_type=MESH)

    def begin_x(s):
        for d in all_far_first:
            for e in range(1, n_ga):
                x_sum(s, e, d).start()

    def begin_z(s):
        for d in all_far_first:
            at = strip_of(flipped(z, d))
            acc = total[s, kept(x), :, at]
            for e in range(1, n_ga):
                x_sum(s, e, d).wait_recv()
                acc = acc + x_in[s, e - 1, :, :, at]
            total[s, kept(x), :, at] = acc
            if d:
                z_sum(s, d).start()

    def begin_sharing(s):
        acc = total[s, kept(x), :, strip_of(z)]
        for d in far_first:
            z_sum(s, d).wait_recv()
            acc = acc + z_in[s, d - 1]
        coef[kept(x), s, :, strip_of(z)] = acc.astype(jnp.bfloat16)
        for e in range(groups - 1, 0, -1):
            if not RELAYED[s] or e % n_ga == 0 or e < n_ga:
                sharing(s, e).start()
        crossing(s).start()

    def relaying(s, e):
        d, e_x = divmod(e, n_ga)
        here = coef.at[kept(x), s, :, strip_of(flipped(z, d))]
        return pltpu.make_async_remote_copy(
            src_ref=here, dst_ref=here,
            send_sem=all_send.at[s, e - 1], recv_sem=all_recv.at[s, e - 1],
            device_id={"ga": flipped(x, e_x)}, device_id_type=MESH)

    def relay(s):
        for d in far_first:
            sharing(s, d * n_ga).wait_recv()
            for e_x in range(1, n_ga):
                relaying(s, d * n_ga + e_x).start()

    def finish_sharing(s):
        for e in range(1, groups):
            if not RELAYED[s] or e < n_ga:
                sharing(s, e).wait()
            elif e % n_ga == 0:
                sharing(s, e).wait_send()
            else:
                relaying(s, e).wait()

    def multiply(g):
        s, k = divmod(g, chunks)
        if s == 0:
            for h in range(2):
                eig_copy(k, h).wait()
        for d in far_first:
            forwarding(g, d).wait_recv()

        def tile(j, carry):
            at = strip_of(j)
            acc = 0.0
            for h in range(2):
                width = widths[k]
                deep = pl.ds(h * reach + starts[k], width)
                left = exch[:, pl.ds(s * part, part), deep].reshape(n * part, width)
                acc += jnp.dot(left, eig[deep, at], preferred_element_type=jnp.float32)
            acc = acc.reshape(n, part, strip)
            if k:
                acc += total[s, :, :, at]
            total[s, :, :, at] = acc
            return carry

        if g < steps - 1:
            lax.fori_loop(0, n, tile, 0)
        else:
            for d in all_far_first:
                tile(flipped(z, d), 0)
                for e in range(1, n_ga):
                    x_sum(s, e, d).start()

    for k in range(chunks):
        for h in range(2):
            eig_copy(k, h).start()
    own_copy().start()

    barrier = pltpu.get_barrier_semaphore()
    for e in range(1, groups):
        pl.semaphore_signal(barrier, inc=1, device_id=peer(e), device_id_type=MESH)
    pl.semaphore_signal(barrier, inc=1, device_id={"sub": 1 - c}, device_id_type=MESH)
    pl.semaphore_signal(
        barrier, inc=1, device_id_type=MESH,
        device_id={"pair": (c * n + z) // n_ga, "ga": (c * n + z) % n_ga, "sub": 1 - c})

    @pl.when(crosses == 1)
    def _():
        for e in range(n_ga):
            pl.semaphore_signal(
                barrier, inc=1, device_id={"pair": rank % n, "ga": e, "sub": 1 - c},
                device_id_type=MESH)

    pl.semaphore_wait(barrier, groups + 1 + n_ga * crosses)

    for g in range(min(AHEAD, steps)):
        for d in far_first:
            sending(g, d).start()
    own_copy().wait()

    after = {}
    for s in range(stages - 1):
        done = (s + 1) * chunks
        gap = max(1, (chunks - 1) // 2)
        after.setdefault(done, []).append((begin_x, s))
        after.setdefault(done + gap, []).append((begin_z, s))
        after.setdefault(done + 2 * gap, []).append((begin_sharing, s))
        if RELAYED[s]:
            after.setdefault(done + 2 * gap + 1, []).append((relay, s))

    for g in range(steps + 1):
        if g < steps:
            for d in far_first:
                sending(g, d).wait_recv()
                forwarding(g, d).start()
            if g + AHEAD < steps:
                for d in far_first:
                    sending(g + AHEAD, d).start()
        if g > 0:
            multiply(g - 1)
        for act, s in after.get(g, []):
            act(s)

    last = stages - 1
    begin_z(last)
    for g in range(steps):
        for d in far_first:
            sending(g, d).wait_send()
            forwarding(g, d).wait_send()
    begin_sharing(last)
    if RELAYED[last]:
        relay(last)
    for s in range(stages):
        for e in range(1, n_ga):
            for d in all_far_first:
                x_sum(s, e, d).wait_send()
        for d in far_first:
            z_sum(s, d).wait_send()
    for s in range(stages):
        finish_sharing(s)

    coef_out[...] = coef[...]
    for s in range(stages):
        crossing(s).wait_send()

    @pl.when(crosses == 0)
    def _():
        block_out[...] = coef[:, :, :, strip_of(rank % n)]

    @pl.when(crosses == 1)
    def _():
        for s in range(stages):
            for e in range(n_ga):
                crossed(s, e).wait_recv()
        block_out[...] = other[...]


def final_kernel(scale, coef, columns, energies, frequencies, out, held, done):
    count, half, width = held.shape
    pairs = coef.shape[0]
    turned = coef[...].T
    energy = jnp.broadcast_to(energies[...], (128, pairs)).T
    squared = energy * energy
    wide = columns[...].astype(jnp.float32)

    def copy(w):
        return pltpu.make_async_copy(held.at[w], out.at[w], done.at[w])

    for w in range(count):
        frequency = frequencies[w]
        factor = 2.0 * energy / (squared + frequency * frequency)
        weighted = [factor * wide[:, i:i + 128] for i in range(0, width, 128)]
        right = jnp.concatenate(weighted, axis=1).astype(jnp.bfloat16)
        held[w] = jnp.dot(turned, right, preferred_element_type=jnp.float32) * scale
        copy(w).start()
    for w in range(count):
        copy(w).wait()


def plain(densities, eigvecs, n, n_ga):
    rows = densities.shape[0]
    _, depth, half = eigvecs.shape
    chunks = depth // WIDTH if depth % WIDTH == 0 else 1
    if depth % 128:
        densities = densities.reshape(rows, n, depth).transpose(1, 0, 2)
    dma = pltpu.SemaphoreType.DMA
    any_space = pl.BlockSpec(memory_space=pl.ANY)
    return pl.pallas_call(
        functools.partial(plain_kernel, n, n_ga),
        out_shape=jax.ShapeDtypeStruct((n * rows, half), jnp.float32),
        in_specs=[any_space, any_space],
        out_specs=pl.BlockSpec(memory_space=pltpu.VMEM),
        scratch_shapes=[
            pltpu.VMEM((depth, half), jnp.bfloat16),
            pltpu.VMEM((n, rows, depth), jnp.bfloat16),
            dma((chunks,)), dma,
        ] + [dma((chunks, n - 1))] * 4,
        compiler_params=pltpu.CompilerParams(
            collective_id=0, has_side_effects=True, vmem_limit_bytes=56 * 1024 * 1024),
    )(densities, eigvecs)


def fused(densities, eigvecs, n, n_ga):
    rows = densities.shape[0]
    _, depth, half = eigvecs.shape
    groups = n * n_ga
    widths = [WIDTH] * ((depth // 2 - sum(LAST_WIDTHS)) // WIDTH) + list(LAST_WIDTHS)
    chunks = len(widths)
    part, block, share = rows // STAGES, 2 * half // groups, n // n_ga
    dma = pltpu.SemaphoreType.DMA
    any_space = pl.BlockSpec(memory_space=pl.ANY)
    vmem = pl.BlockSpec(memory_space=pltpu.VMEM)
    coef_shape, block_shape = (n, STAGES, part, half), (n, STAGES, part, block)
    coef, columns = pl.pallas_call(
        functools.partial(fused_kernel, n, n_ga, widths),
        out_shape=(
            jax.ShapeDtypeStruct(coef_shape, jnp.bfloat16),
            jax.ShapeDtypeStruct(block_shape, jnp.bfloat16),
        ),
        in_specs=[any_space, any_space],
        out_specs=(vmem, vmem),
        scratch_shapes=[
            pltpu.VMEM((depth, half), jnp.bfloat16),
            pltpu.VMEM((n, rows, depth), jnp.bfloat16),
            pltpu.VMEM((STAGES, n, part, half), jnp.float32),
            pltpu.VMEM((STAGES, n_ga - 1, share, part, half), jnp.float32),
            pltpu.VMEM((STAGES, n - 1, share, part, half // n), jnp.float32),
            pltpu.VMEM(coef_shape, jnp.bfloat16),
            pltpu.VMEM(block_shape, jnp.bfloat16),
            dma((chunks, 2)), dma,
        ] + [dma((STAGES * chunks, n - 1))] * 4 + [
            dma((STAGES, n_ga - 1, n)), dma((STAGES, n_ga - 1, n)),
            dma((STAGES, n - 1)), dma((STAGES, n - 1)),
            dma((STAGES, groups - 1)), dma((STAGES, groups - 1)),
            dma((STAGES,)), dma((STAGES, n_ga)),
        ],
        compiler_params=pltpu.CompilerParams(
            collective_id=0, has_side_effects=True, vmem_limit_bytes=56 * 1024 * 1024),
        cost_estimate=pl.CostEstimate(
            flops=2 * n * rows * depth * half, transcendentals=0,
            bytes_accessed=2 * depth * (half + n * rows)),
    )(densities, eigvecs)
    return coef.reshape(n * rows, half), columns.reshape(n * rows, block)


def final(coef, columns, energies, frequencies):
    pairs, half = coef.shape
    block = columns.shape[1]
    count = frequencies.shape[0]
    vmem = pl.BlockSpec(memory_space=pltpu.VMEM)
    return pl.pallas_call(
        functools.partial(final_kernel, -1.0 / pairs),
        out_shape=jax.ShapeDtypeStruct((count, half, block), jnp.float32),
        in_specs=[vmem, vmem, vmem, pl.BlockSpec(memory_space=pltpu.SMEM)],
        out_specs=pl.BlockSpec(memory_space=pl.ANY),
        scratch_shapes=[
            pltpu.VMEM((count, half, block), jnp.float32), pltpu.SemaphoreType.DMA((count,)),
        ],
        compiler_params=pltpu.CompilerParams(vmem_limit_bytes=16 * 1024 * 1024),
    )(coef, columns, energies.reshape(1, pairs), frequencies)


def on_device(densities, eigvecs, energies, frequencies):
    n, n_ga = lax.axis_size("pair"), lax.axis_size("ga")
    rows, depth, half = densities.shape[0], eigvecs.shape[1], eigvecs.shape[2]
    groups = n * n_ga
    fits = (
        depth % 256 == 0 and depth // 2 % WIDTH == sum(LAST_WIDTHS) % WIDTH
        and depth // 2 > sum(LAST_WIDTHS) and rows % (16 * STAGES) == 0 and n % n_ga == 0
        and half % (128 * n) == 0 and n_ga == 2
    )
    if fits:
        coefficients, columns = fused(densities, eigvecs, n, n_ga)
        return final(coefficients, columns, energies, frequencies)
    partial_value = plain(densities, eigvecs, n, n_ga)
    coefficients = lax.psum(partial_value, ("pair", "ga")).astype(jnp.bfloat16)
    width = 2 * half // groups
    start = (lax.axis_index("pair") * n_ga + lax.axis_index("ga")) * width
    swapped = lax.ppermute(coefficients, "sub", [(0, 1), (1, 0)])
    first = lax.axis_index("sub") == 0
    whole = jnp.concatenate(
        [jnp.where(first, coefficients, swapped), jnp.where(first, swapped, coefficients)], axis=1)
    columns = lax.dynamic_slice_in_dim(whole, start, width, 1)
    squared = energies * energies
    factor = (
        2.0 * energies[None, :] / (squared[None, :] + frequencies[:, None] * frequencies[:, None])
    )
    weighted = (factor[:, :, None] * columns.astype(jnp.float32)[None, :, :]).astype(jnp.bfloat16)
    result = jnp.einsum("ps,wpt->wst", coefficients, weighted, preferred_element_type=jnp.float32)
    return result * (-1.0 / (n * rows))


def solution(mesh):
    placed = (P(("grp", "pair"), "ga"), P("ga", "pair", "sub"), P("grp"), P())
    return jax.shard_map(
        on_device,
        mesh=mesh,
        in_specs=placed,
        out_specs=P("grp", "sub", ("pair", "ga")),
        check_vma=False,
    )
```
